32 devices in a mesh: groups: 2 (over y), gx: 8 (over z, x), gy: 2 (over core).
Axes of the slice: x: 2, y: 2, z: 4, core: 2. Of those that a mesh axis runs over, the one named last changes fastest.
Arguments:
- residual: bfloat16 [128, 16384], P(('groups', 'gx'), 'gy'), parts along dimension 0, may hold values from -6 to 6
- query: bfloat16 [128, 16384], P('groups', ('gx', 'gy')), parts along dimension 0, may hold values from -6 to 6
- new_keyval: bfloat16 [128, 2048], P('groups', ('gx', 'gy')), parts along dimension 0, may hold values from -6 to 6
- key_cache: bfloat16 [128, 512, 1024], P(('groups', 'gx', 'gy')), parts along dimension 0, may hold values from -1000 to 1000
- value_cache: bfloat16 [128, 512, 1024], P(('groups', 'gx', 'gy')), parts along dimension 0, may hold values from -6 to 6
- lengths: int32 [128], P(('groups', 'gx', 'gy')), parts along dimension 0, may hold values from 1 to 511, as said below
- out_weight: bfloat16 [16384, 16384], P('gx', 'gy'), may hold values from -0.046875 to 0.046875
Outputs:
- layer_out: bfloat16 [128, 16384], P(('groups', 'gx'), 'gy'), parts along dimension 0
The draws below stay inside these ranges and needn't reach their ends.
There are 2 independent parts, one for each index of `groups`. The reference program is written for one: setup_inputs(seed, part) draws one part's arguments, and reference() takes and returns one part's arrays. A program takes and returns all parts, laid end to end along the dimension named above; an argument that names none is the same for every part. Nothing has to cross between parts.
Inputs may be any that keep to these rules, and one draw needn't show every extreme that they name: Each request's new token takes position lengths[r]; positions 0 to lengths[r] are attended; one request has 511.
All inputs are finite; a program needn't handle non-finite values.
Results may differ from the reference program's by a relative error of at most 0.007.
The reference program's roundings to bfloat16 on the way (of `rope_query`, `new_key`, `key_rows`, `weights`, `attended` and `mixed`) count: a program that leaves them out, or rounds other values in their place, can miss the bound.
Values may be sent and summed in bfloat16 or wider, within the bound.
No kernel may reach another device: no remote copies, remote signals or barrier semaphores. Data moves between devices by JAX's collectives and lax.ppermute only.
A program may use at most 128 MiB of HBM per device.

```python
import math
import jax
import jax.numpy as jnp
from jax import lax

D = 16384
HEADS = 128
KV_HEADS = 8
HD = 128
MAXLEN = 512
BATCH = 64


def draw_lengths(key, part):
    key = jax.random.fold_in(key, 11)
    first_key, second_key = jax.random.split(key)
    drawn = jax.random.randint(first_key, (BATCH,), 1, MAXLEN, dtype=jnp.int32)
    chosen = jax.random.randint(second_key, (), 0, BATCH, dtype=jnp.int32)
    return jnp.where(jnp.arange(BATCH, dtype=jnp.int32) == chosen, MAXLEN - 1, drawn)


def draw_key_cache(key, part):
    key = jax.random.fold_in(key, 23)
    first_key = jax.random.fold_in(key, 0)
    drawn = jax.random.normal(first_key, (BATCH, MAXLEN, KV_HEADS * HD), jnp.float32)
    return jnp.clip(drawn, -1000.0, 1000.0).astype(jnp.bfloat16)


def block_scale(own_key, dims, cuts, least, high):
    def one(dim, blocks):
        draws = jax.random.uniform(jax.random.fold_in(jax.random.fold_in(own_key, 6), dim), (blocks,), jnp.float32, least / len(cuts), high / len(cuts))
        return jnp.repeat(jnp.exp(draws), dims[dim] // blocks).reshape((-1,) + (1,) * (len(dims) - dim - 1))

    level = one(*cuts[0])
    for cut in cuts[1:]:
        level = level * one(*cut)
    return level


def bell_draw(rng, dims, spread, reach, cuts=(), held_as=jnp.bfloat16):
    values = spread * jax.random.normal(rng, dims, jnp.float32)
    if cuts:
        values = values * block_scale(rng, dims, cuts, -0.22, 0.18)
    return jnp.clip(values, -reach, reach).astype(held_as)


def setup_inputs(seed: int = 0, part: int = 0) -> dict:
    key_list = jax.random.split(jax.random.key(seed), 8)
    part_splits = jax.random.split(jax.random.fold_in(key_list[7], part), 8)
    return {
        "residual": bell_draw(part_splits[0], (BATCH, D), 1.0, 6.0, ((0, 8), (1, 2))),
        "query": bell_draw(part_splits[1], (BATCH, HEADS * HD), 1.0, 6.0, ((1, 16),)),
        "new_keyval": bell_draw(part_splits[2], (BATCH, 2 * KV_HEADS * HD), 1.0, 6.0, ((1, 16),)),
        "key_cache": draw_key_cache(jax.random.fold_in(jax.random.fold_in(key_list[7], part), 71), part),
        "value_cache": bell_draw(part_splits[4], (BATCH, MAXLEN, KV_HEADS * HD), 1.0, 6.0, ((0, 16),)),
        "lengths": draw_lengths(jax.random.fold_in(jax.random.fold_in(key_list[7], part), 71), part),
        "out_weight": bell_draw(key_list[6], (HEADS * HD, D), (HEADS * HD) ** -0.5, 0.046875, ((0, 8), (1, 2))),
    }


rope_base = 500000.0

def sign_entries(row_index, col_index, matrix_order):
    anded = jnp.bitwise_and(row_index[:, None], col_index[None, :])
    parity = jnp.zeros(anded.shape, jnp.int32)
    for bit_index in range(int(matrix_order).bit_length()):
        parity = parity + jnp.bitwise_and(jnp.right_shift(anded, bit_index), 1)
    signs = 1.0 - 2.0 * jnp.bitwise_and(parity, 1).astype(jnp.float32)
    return signs / math.sqrt(matrix_order)

def sylvester(matrix_order):
    ladder = jnp.arange(matrix_order, dtype=jnp.int32)
    return sign_entries(ladder, ladder, matrix_order)

def rotary(vector, position):
    half_dim = vector.shape[-1] // 2
    frequency = rope_base ** (-2.0 * jnp.arange(half_dim, dtype=jnp.float32) / vector.shape[-1])
    angles = position[:, None] * frequency[None, :]
    angles = jnp.concatenate([angles, angles], axis=-1)[:, None, :]
    turned = jnp.concatenate([-vector[..., half_dim:], vector[..., :half_dim]], axis=-1)
    return vector * jnp.cos(angles) + turned * jnp.sin(angles)

def rotate_heads(vector, head_table):
    return jnp.einsum('rhd,de->rhe', vector, head_table, precision=lax.Precision.HIGHEST)

def reference(residual, query, new_keyval, key_cache, value_cache, lengths, out_weight):
    head_table = sylvester(HD)
    position = lengths.astype(jnp.float32)
    rope_query = rotate_heads(rotary(query.astype(jnp.float32).reshape(BATCH, HEADS, HD), position), head_table)
    rope_query = rope_query.astype(jnp.bfloat16)
    key_value = new_keyval.reshape(BATCH, 2, KV_HEADS, HD)
    new_key = rotate_heads(rotary(key_value[:, 0].astype(jnp.float32), position), head_table).astype(jnp.bfloat16)
    new_value = key_value[:, 1]
    group_size = HEADS // KV_HEADS
    slot_index = jnp.arange(MAXLEN, dtype=jnp.int32)

    def one_row(row_items):
        query_row, key_row, value_row, key_block, value_block, length = row_items
        current = (slot_index == length)[:, None, None]
        key_rows = jnp.where(current, key_row[None], key_block.reshape(MAXLEN, KV_HEADS, HD))
        value_rows = jnp.where(current, value_row[None], value_block.reshape(MAXLEN, KV_HEADS, HD))
        grouped = query_row.astype(jnp.float32).reshape(KV_HEADS, group_size, HD)
        scores = jnp.einsum('kgd,pkd->kgp', grouped, key_rows.astype(jnp.float32)) / math.sqrt(HD)
        scores = jnp.where((slot_index <= length)[None, None, :], scores, -jnp.inf)
        row_max = lax.optimization_barrier(jnp.max(scores, axis=-1, keepdims=True))
        weights = jnp.exp(scores - row_max)
        weights = (weights / lax.optimization_barrier(jnp.sum(weights, axis=-1, keepdims=True))).astype(jnp.bfloat16)
        attended = jnp.einsum('kgp,pkd->kgd', weights.astype(jnp.float32), value_rows.astype(jnp.float32))
        return attended.reshape(HEADS, HD).astype(jnp.bfloat16)
    attended = lax.map(one_row, (rope_query, new_key, new_value, key_cache, value_cache, lengths))
    mixing = sylvester(HEADS)
    mixed = jnp.einsum('gh,rhd->rgd', mixing, attended.astype(jnp.float32), precision=lax.Precision.HIGHEST)
    mixed = mixed.astype(jnp.bfloat16).reshape(BATCH, HEADS * HD)
    projected = jnp.dot(mixed, out_weight, preferred_element_type=jnp.float32)
    return (residual.astype(jnp.float32) + projected).astype(jnp.bfloat16)
```

```python
import math

import jax
import jax.numpy as jnp
from jax import lax
from jax.sharding import PartitionSpec as P

HEADS = 128
KV_HEADS = 8
HD = 128


rope_base = 500000.0


def sign_entries(row_index, col_index, matrix_order):
    anded = jnp.bitwise_and(row_index[:, None], col_index[None, :])
    parity = jnp.zeros(anded.shape, jnp.int32)
    for bit_index in range(int(matrix_order).bit_length()):
        parity = parity + jnp.bitwise_and(jnp.right_shift(anded, bit_index), 1)
    signs = 1.0 - 2.0 * jnp.bitwise_and(parity, 1).astype(jnp.float32)
    return signs / math.sqrt(matrix_order)


def sylvester(matrix_order):
    ladder = jnp.arange(matrix_order, dtype=jnp.int32)
    return sign_entries(ladder, ladder, matrix_order)


def rotary(vector, position):
    half_dim = vector.shape[-1] // 2
    frequency = rope_base ** (-2.0 * jnp.arange(half_dim, dtype=jnp.float32) / vector.shape[-1])
    angles = position[:, None] * frequency[None, :]
    angles = jnp.concatenate([angles, angles], axis=-1)[:, None, :]
    turned = jnp.concatenate([-vector[..., half_dim:], vector[..., :half_dim]], axis=-1)
    return vector * jnp.cos(angles) + turned * jnp.sin(angles)


def rotate_heads(vector, head_table):
    return jnp.einsum("rhd,de->rhe", vector, head_table, precision=lax.Precision.HIGHEST)


def mix_local(attended):
    mixing = sylvester(HEADS)
    mixed = jnp.einsum(
        "gh,rhd->rgd", mixing, attended.astype(jnp.float32), precision=lax.Precision.HIGHEST
    )
    return mixed.astype(jnp.bfloat16)


def shards(residual, query, new_keyval, key_cache, value_cache, lengths, out_weight):
    gx_count = lax.axis_size("gx")
    row_count = lengths.shape[0]
    max_slots = key_cache.shape[1]
    group_size = HEADS // KV_HEADS
    query_width = query.shape[1]
    fused_rows = jnp.concatenate([query, new_keyval], axis=1).reshape(-1, row_count, query_width + new_keyval.shape[1])
    fused_rows = lax.all_to_all(fused_rows, ("gx", "gy"), split_axis=0, concat_axis=0, tiled=True)
    fused_rows = fused_rows.transpose(1, 0, 2)
    query_rows = fused_rows[:, :, :query_width].reshape(row_count, -1)
    keyval_rows = fused_rows[:, :, query_width:].reshape(row_count, -1)
    head_table = sylvester(HD)
    position = lengths.astype(jnp.float32)
    rope_query = rotate_heads(
        rotary(query_rows.astype(jnp.float32).reshape(row_count, HEADS, HD), position), head_table
    )
    rope_query = rope_query.astype(jnp.bfloat16)
    key_value = keyval_rows.reshape(row_count, 2, KV_HEADS, HD)
    new_key = rotate_heads(
        rotary(key_value[:, 0].astype(jnp.float32), position), head_table
    ).astype(jnp.bfloat16)
    new_value = key_value[:, 1]
    slot_index = jnp.arange(max_slots, dtype=jnp.int32)
    current = (slot_index[None, :] == lengths[:, None])[:, :, None, None]
    key_rows = jnp.where(
        current, new_key[:, None], key_cache.reshape(row_count, max_slots, KV_HEADS, HD)
    )
    value_rows = jnp.where(
        current, new_value[:, None], value_cache.reshape(row_count, max_slots, KV_HEADS, HD)
    )
    grouped = rope_query.reshape(row_count, KV_HEADS, group_size, HD)
    scores = jnp.einsum(
        "rkgd,rpkd->rkgp", grouped, key_rows, preferred_element_type=jnp.float32
    ) / math.sqrt(HD)
    visible = (slot_index[None, :] <= lengths[:, None])[:, None, None, :]
    scores = jnp.where(visible, scores, -jnp.inf)
    row_max = jnp.max(scores, axis=-1, keepdims=True)
    weights = jnp.exp(scores - row_max)
    weights = (weights / jnp.sum(weights, axis=-1, keepdims=True)).astype(jnp.bfloat16)
    attended = jnp.einsum(
        "rkgp,rpkd->rkgd", weights, value_rows, preferred_element_type=jnp.float32
    )
    attended = attended.astype(jnp.bfloat16).reshape(row_count, HEADS, HD)
    feature_width = HEADS * HD // gx_count
    head_major = mix_local(attended)
    pieces_in = lax.all_to_all(
        head_major.reshape(1, 1, row_count, gx_count, feature_width),
        "gx",
        split_axis=3,
        concat_axis=0,
        tiled=True,
    )
    gathered = lax.all_gather(pieces_in, "gy", axis=1, tiled=True)
    feature_rows = gathered.reshape(-1, feature_width)
    partial = jnp.dot(feature_rows, out_weight, preferred_element_type=jnp.float32)
    partial = partial.astype(jnp.bfloat16).reshape(gx_count, -1, out_weight.shape[1])
    terms = lax.all_to_all(partial, "gx", split_axis=0, concat_axis=0, tiled=True)
    summed = jnp.sum(terms.astype(jnp.float32), axis=0)
    return (residual.astype(jnp.float32) + summed).astype(jnp.bfloat16)


def solution(mesh):
    in_specs = (
        P(("groups", "gx"), "gy"),
        P("groups", ("gx", "gy")),
        P("groups", ("gx", "gy")),
        P(("groups", "gx", "gy"), None, None),
        P(("groups", "gx", "gy"), None, None),
        P(("groups", "gx", "gy")),
        P("gx", "gy"),
    )
    out_specs = P(("groups", "gx"), "gy")
    return jax.shard_map(shards, mesh=mesh, in_specs=in_specs, out_specs=out_specs, check_vma=False)
```

```python
import functools
import math

import jax
import jax.numpy as jnp
import numpy as np
from jax import lax
from jax.experimental import pallas as pl
from jax.experimental.pallas import tpu as pltpu
from jax.sharding import PartitionSpec as P

HEADS = 128
KV_HEADS = 8
HD = 128
GROUP = HEADS // KV_HEADS
ROPE_BASE = 500000.0
NORM = 1.0 / math.sqrt(HD)
MIX_NORM = 1.0 / math.sqrt(HEADS)
CHUNKS = (0.5, 0.5)
NEAR = 4
TILE = 512


def sign_table(order):
    bits = lax.broadcasted_iota(jnp.int32, (order, order), 0) & lax.broadcasted_iota(jnp.int32, (order, order), 1)
    step = 1
    while step < order.bit_length():
        step *= 2
    while step > 1:
        step //= 2
        bits = bits ^ (bits >> step)
    return (1 - 2 * (bits & 1)).astype(jnp.float32).astype(jnp.bfloat16)


def hadamard(rows, table):
    high = rows.astype(jnp.bfloat16)
    rest = rows - high.astype(jnp.float32)
    middle = rest.astype(jnp.bfloat16)
    low = (rest - middle.astype(jnp.float32)).astype(jnp.bfloat16)
    dot = functools.partial(jnp.dot, preferred_element_type=jnp.float32)
    return (dot(high, table) + (dot(middle, table) + dot(low, table))) * NORM


def put_row(buf, r, length, rows):
    base = pl.multiple_of((length >> 4) << 4, 16)
    here = lax.broadcasted_iota(jnp.int32, (16, HD), 0) == length - base
    for k in range(KV_HEADS):
        lanes = slice(k * HD, (k + 1) * HD)
        old = buf[r, pl.ds(base, 16), lanes].astype(jnp.float32)
        buf[r, pl.ds(base, 16), lanes] = jnp.where(here, rows[k:k + 1], old).astype(jnp.bfloat16)


def attend(
    lengths_ref, query_ref, keyval_ref, turn_ref, key_hbm, value_hbm,
    out_ref, key_buf, value_buf, key_sem, value_sem,
):
    row_count, slots = key_buf.shape[:2]
    copies = []
    for r in range(row_count):
        pair = (
            pltpu.make_async_copy(key_hbm.at[r], key_buf.at[r], key_sem.at[r]),
            pltpu.make_async_copy(value_hbm.at[r], value_buf.at[r], value_sem.at[r]),
        )
        for copy in pair:
            copy.start()
        copies.append(pair)
    table = sign_table(HD)
    turned = []
    for r in range(row_count):
        cos, sin = turn_ref[r, 0:1, :], turn_ref[r, 1:2, :]
        for vector in (query_ref[r].astype(jnp.float32), keyval_ref[r].astype(jnp.float32)):
            turned.append(vector * cos + pltpu.roll(vector, HD // 2, axis=1) * sin)
    turned = hadamard(jnp.concatenate(turned, axis=0), table)
    stride = HEADS + 2 * KV_HEADS
    head_of = lax.broadcasted_iota(jnp.int32, (HD, HEADS), 1) // GROUP
    slot = lax.broadcasted_iota(jnp.int32, (slots, HEADS), 0)
    for r in range(row_count):
        length = lengths_ref[r]
        across = jnp.transpose(turned[r * stride:r * stride + HEADS])
        spread = jnp.concatenate(
            [jnp.where(head_of == k, across, 0.0).astype(jnp.bfloat16) for k in range(KV_HEADS)], axis=0
        )
        copies[r][0].wait()
        new_key = turned[r * stride + HEADS:r * stride + HEADS + KV_HEADS]
        put_row(key_buf, r, length, new_key)
        scores = jnp.dot(key_buf[r], spread, preferred_element_type=jnp.float32) * NORM
        scores = jnp.where(slot <= length, scores, -jnp.inf)
        weights = jnp.exp(scores - jnp.max(scores, axis=0, keepdims=True))
        weights = weights * (1.0 / jnp.sum(weights, axis=0, keepdims=True))
        weights = jnp.transpose(weights).astype(jnp.bfloat16)
        copies[r][1].wait()
        put_row(value_buf, r, length, keyval_ref[r, KV_HEADS:].astype(jnp.float32))
        attended = []
        for k in range(0, KV_HEADS, 2):
            two = jnp.dot(
                weights[k * GROUP:(k + 2) * GROUP], value_buf[r, :, k * HD:(k + 2) * HD],
                preferred_element_type=jnp.float32,
            )
            attended += [two[:GROUP, :HD], two[GROUP:, HD:]]
        attended = jnp.concatenate(attended, axis=0).astype(jnp.bfloat16)
        mixed = jnp.dot(table, attended, preferred_element_type=jnp.float32) * MIX_NORM
        out_ref[:, r] = mixed.reshape(out_ref.shape[0], *out_ref.shape[2:]).astype(jnp.bfloat16)


def attention(lengths, query, keyval, turn, key_cache, value_cache, blocks):
    row_count, slots, width = key_cache.shape
    vmem, hbm = pl.BlockSpec(memory_space=pltpu.VMEM), pl.BlockSpec(memory_space=pltpu.HBM)
    key_cache = pltpu.with_memory_space_constraint(key_cache, pltpu.HBM)
    value_cache = pltpu.with_memory_space_constraint(value_cache, pltpu.HBM)
    return pl.pallas_call(
        attend,
        out_shape=jax.ShapeDtypeStruct((blocks, row_count, HEADS // blocks, HD), jnp.bfloat16),
        in_specs=[pl.BlockSpec(memory_space=pltpu.SMEM)] + [vmem] * 3 + [hbm] * 2,
        out_specs=vmem,
        scratch_shapes=[
            pltpu.VMEM((row_count, slots, width), jnp.bfloat16),
            pltpu.VMEM((row_count, slots, width), jnp.bfloat16),
            pltpu.SemaphoreType.DMA((row_count,)),
            pltpu.SemaphoreType.DMA((row_count,)),
        ],
        compiler_params=pltpu.CompilerParams(vmem_limit_bytes=32 * 2**20),
        cost_estimate=pl.CostEstimate(
            flops=4 * row_count * HEADS * slots * HD,
            bytes_accessed=4 * row_count * slots * width,
            transcendentals=row_count * HEADS * slots,
        ),
        name="attend",
    )(lengths, query, keyval, turn, key_cache, value_cache)


def project(first, place_ref, rows_ref, weight_hbm, own_ref, *rest):
    send_refs, (product_ref, weight_buf, weight_sem) = rest[:-3], rest[-3:]
    blocks = product_ref.shape[0]
    tiles = weight_buf.shape[0]
    copies = []
    for j in range(tiles):
        columns = pl.ds((first + j) * TILE, TILE)
        copies.append(pltpu.make_async_copy(weight_hbm.at[:, columns], weight_buf.at[j], weight_sem.at[j]))
        copies[-1].start()
    place = place_ref[0]
    for j in range(tiles):
        columns = slice(j * TILE, (j + 1) * TILE)
        copies[j].wait()
        product = jnp.dot(rows_ref[...], weight_buf[j], preferred_element_type=jnp.float32)
        product_ref[:, :, columns] = product.reshape(blocks, -1, TILE)
        for step in range(NEAR):
            taken = jnp.concatenate(
                [product_ref[NEAR * far + (place ^ step), :, columns] for far in range(blocks // NEAR)], axis=0
            )
            if step:
                send_refs[step - 1][:, columns] = taken.astype(jnp.bfloat16)
            else:
                own_ref[:, columns] = taken


def projection(place, rows, weight, first, count, blocks):
    row_count, depth = rows.shape
    out_rows = row_count // NEAR
    vmem = pl.BlockSpec(memory_space=pltpu.VMEM)
    shapes = [jax.ShapeDtypeStruct((out_rows, count * TILE), jnp.float32)]
    shapes += [jax.ShapeDtypeStruct((out_rows, count * TILE), jnp.bfloat16)] * (NEAR - 1)
    return pl.pallas_call(
        functools.partial(project, first),
        out_shape=shapes,
        in_specs=[pl.BlockSpec(memory_space=pltpu.SMEM), vmem, pl.BlockSpec(memory_space=pltpu.HBM)],
        out_specs=[vmem] * NEAR,
        scratch_shapes=[
            pltpu.VMEM((blocks, row_count // blocks, count * TILE), jnp.float32),
            pltpu.VMEM((count, depth, TILE), jnp.bfloat16),
            pltpu.SemaphoreType.DMA((count,)),
        ],
        compiler_params=pltpu.CompilerParams(vmem_limit_bytes=40 * 2**20),
        cost_estimate=pl.CostEstimate(
            flops=2 * row_count * depth * count * TILE,
            bytes_accessed=2 * depth * count * TILE,
            transcendentals=0,
        ),
        name="project",
    )(place, rows, pltpu.with_memory_space_constraint(weight, pltpu.HBM))


def shards(residual, query, new_keyval, key_cache, value_cache, lengths, out_weight):
    gx_count = lax.axis_size("gx")
    gx_index = lax.axis_index("gx")
    row_count = lengths.shape[0]
    query_width = query.shape[1]

    both = jnp.concatenate([query, new_keyval], axis=1).reshape(-1, row_count, query_width + new_keyval.shape[1])
    both = lax.all_to_all(both, ("gx", "gy"), split_axis=0, concat_axis=0, tiled=True)
    both = both.transpose(1, 0, 2)
    query_rows = both[:, :, :query_width].reshape(row_count, HEADS, HD)
    keyval_rows = both[:, :, query_width:].reshape(row_count, 2 * KV_HEADS, HD)

    frequency = ROPE_BASE ** (-2.0 * np.arange(HD // 2) / HD)
    frequency = np.concatenate([frequency, frequency]).astype(np.float32)
    side = np.where(np.arange(HD) < HD // 2, -1.0, 1.0).astype(np.float32)
    angles = lengths.astype(jnp.float32)[:, None] * frequency[None, :]
    turn = jnp.stack([jnp.cos(angles), jnp.sin(angles) * side], axis=1)

    bounded = jnp.minimum(lengths, key_cache.shape[1] - 1)
    mixed = attention(bounded, query_rows, keyval_rows, turn, key_cache, value_cache, gx_count)
    mixed = lax.all_to_all(mixed, "gx", split_axis=0, concat_axis=0, tiled=True)
    mixed = lax.all_gather(mixed, "gy", axis=1)
    feature_rows = mixed.reshape(gx_count * 2 * row_count, -1)

    near_place = jnp.reshape(gx_index % NEAR, (1,)).astype(jnp.int32)
    far_count = gx_count // NEAR
    far_place = gx_index // NEAR
    block_rows = feature_rows.shape[0] // gx_count
    tiles = out_weight.shape[1] // TILE
    outs = []
    first = 0
    for share in CHUNKS:
        count = int(round(tiles * share))
        columns = slice(first * TILE, (first + count) * TILE)
        own, *sends = projection(near_place, feature_rows, out_weight, first, count, gx_count)
        total = own
        for step, send in enumerate(sends, 1):
            got = lax.ppermute(send, "gx", [(i, i ^ step) for i in range(gx_count)])
            total = total + got.astype(jnp.float32)
        total = total.reshape(far_count, block_rows, count * TILE)
        if far_count == 2:
            low, high = total[0], total[1]
            mine = jnp.where(far_place == 0, low, high)
            send = jnp.where(far_place == 0, high, low).astype(jnp.bfloat16)
            got = lax.ppermute(send, "gx", [(i, i ^ NEAR) for i in range(gx_count)])
            summed = mine + got.astype(jnp.float32)
        elif far_count > 1:
            parts = [[near + NEAR * far for far in range(far_count)] for near in range(NEAR)]
            got = lax.all_to_all(
                total.astype(jnp.bfloat16), "gx", split_axis=0, concat_axis=0,
                axis_index_groups=parts, tiled=True,
            )
            summed = jnp.sum(got.astype(jnp.float32), axis=0)
        else:
            summed = total[0]
        outs.append((residual[:, columns].astype(jnp.float32) + summed).astype(jnp.bfloat16))
        first += count
    return jnp.concatenate(outs, axis=1)


def solution(mesh):
    in_specs = (
        P(("groups", "gx"), "gy"),
        P("groups", ("gx", "gy")),
        P("groups", ("gx", "gy")),
        P(("groups", "gx", "gy"), None, None),
        P(("groups", "gx", "gy"), None, None),
        P(("groups", "gx", "gy")),
        P("gx", "gy"),
    )
    out_specs = P(("groups", "gx"), "gy")
    return jax.shard_map(shards, mesh=mesh, in_specs=in_specs, out_specs=out_specs, check_vma=False)
```

```python
import functools
import math

import jax
import jax.numpy as jnp
import numpy as np
from jax import lax
from jax.experimental import pallas as pl
from jax.experimental.pallas import tpu as pltpu
from jax.sharding import PartitionSpec as P

HEADS = 128
KV_HEADS = 8
HD = 128
GROUP = HEADS // KV_HEADS
ROPE_BASE = 500000.0
NORM = 1.0 / math.sqrt(HD)
MIX_NORM = 1.0 / math.sqrt(HEADS)
CHUNKS = (0.375, 0.625)
NEAR = 4
TILE = 512
LEAD = 4


def sign_table(order):
    bits = lax.broadcasted_iota(jnp.int32, (order, order), 0) & lax.broadcasted_iota(jnp.int32, (order, order), 1)
    step = 1
    while step < order.bit_length():
        step *= 2
    while step > 1:
        step //= 2
        bits = bits ^ (bits >> step)
    return (1 - 2 * (bits & 1)).astype(jnp.float32).astype(jnp.bfloat16)


def hadamard(rows, table):
    high = rows.astype(jnp.bfloat16)
    rest = rows - high.astype(jnp.float32)
    middle = rest.astype(jnp.bfloat16)
    low = (rest - middle.astype(jnp.float32)).astype(jnp.bfloat16)
    dot = functools.partial(jnp.dot, preferred_element_type=jnp.float32)
    return (dot(high, table) + (dot(middle, table) + dot(low, table))) * NORM


def put_row(buf, length, rows):
    base = pl.multiple_of((length >> 4) << 4, 16)
    here = lax.broadcasted_iota(jnp.int32, (16, HD), 0) == length - base
    for k in range(KV_HEADS):
        lanes = slice(k * HD, (k + 1) * HD)
        old = buf[pl.ds(base, 16), lanes].astype(jnp.float32)
        buf[pl.ds(base, 16), lanes] = jnp.where(here, rows[k:k + 1], old).astype(jnp.bfloat16)


def attend(
    first, lengths_ref, query_ref, keyval_ref, turn_ref, key_hbm, value_hbm, weight_hbm,
    out_ref, lead_ref, *scratch,
):
    row_count = lengths_ref.shape[0]
    key_bufs, value_bufs = scratch[:row_count], scratch[row_count:2 * row_count]
    sem = scratch[-1]
    slots = key_bufs[0].shape[0]
    requests = range(row_count)
    key_copies = [pltpu.make_async_copy(key_hbm.at[r], key_bufs[r], sem.at[r]) for r in requests]
    value_copies = [pltpu.make_async_copy(value_hbm.at[r], value_bufs[r], sem.at[row_count + r]) for r in requests]
    lead_copies = [
        pltpu.make_async_copy(
            weight_hbm.at[:, pl.ds((first + j) * TILE, TILE)], lead_ref.at[j], sem.at[2 * row_count + j]
        )
        for j in range(lead_ref.shape[0])
    ]
    for copy in key_copies + value_copies + lead_copies:
        copy.start()
    table = sign_table(HD)
    turned = []
    for r in requests:
        cos, sin = turn_ref[r, 0:1, :], turn_ref[r, 1:2, :]
        for vector in (query_ref[r].astype(jnp.float32), keyval_ref[r].astype(jnp.float32)):
            turned.append(vector * cos + pltpu.roll(vector, HD // 2, axis=1) * sin)
    turned = hadamard(jnp.concatenate(turned, axis=0), table)
    stride = HEADS + 2 * KV_HEADS
    head_of = lax.broadcasted_iota(jnp.int32, (HD, HEADS), 1) // GROUP
    spread = []
    for r in requests:
        across = jnp.transpose(turned[r * stride:r * stride + HEADS])
        spread.append(jnp.concatenate(
            [jnp.where(head_of == k, across, 0.0).astype(jnp.bfloat16) for k in range(KV_HEADS)], axis=0
        ))
    for r in requests:
        key_copies[r].wait()
        put_row(key_bufs[r], lengths_ref[r], turned[r * stride + HEADS:r * stride + HEADS + KV_HEADS])
    slot = lax.broadcasted_iota(jnp.int32, (slots, HEADS), 0)
    weights = []
    for r in requests:
        scores = jnp.dot(key_bufs[r][...], spread[r], preferred_element_type=jnp.float32) * NORM
        scores = jnp.where(slot <= lengths_ref[r], scores, -jnp.inf)
        lifted = jnp.exp(scores - jnp.max(scores, axis=0, keepdims=True))
        lifted = lifted * (1.0 / jnp.sum(lifted, axis=0, keepdims=True))
        weights.append(jnp.transpose(lifted.astype(jnp.bfloat16)))
    for r in requests:
        value_copies[r].wait()
        put_row(value_bufs[r], lengths_ref[r], keyval_ref[r, KV_HEADS:].astype(jnp.float32))
    for r in requests:
        attended = []
        for k in range(0, KV_HEADS, 2):
            two = jnp.dot(
                weights[r][k * GROUP:(k + 2) * GROUP], value_bufs[r][:, k * HD:(k + 2) * HD],
                preferred_element_type=jnp.float32,
            )
            attended += [two[:GROUP, :HD], two[GROUP:, HD:]]
        attended = jnp.concatenate(attended, axis=0).astype(jnp.bfloat16)
        mixed = jnp.dot(table, attended, preferred_element_type=jnp.float32) * MIX_NORM
        out_ref[:, r] = mixed.reshape(out_ref.shape[0], *out_ref.shape[2:]).astype(jnp.bfloat16)
    for copy in lead_copies:
        copy.wait()


def attention(lengths, query, keyval, turn, key_cache, value_cache, weight, first, blocks):
    row_count, slots, width = key_cache.shape
    vmem, hbm = pl.BlockSpec(memory_space=pltpu.VMEM), pl.BlockSpec(memory_space=pltpu.HBM)
    key_cache = pltpu.with_memory_space_constraint(key_cache, pltpu.HBM)
    value_cache = pltpu.with_memory_space_constraint(value_cache, pltpu.HBM)
    weight = pltpu.with_memory_space_constraint(weight, pltpu.HBM)
    return pl.pallas_call(
        functools.partial(attend, first),
        out_shape=(
            jax.ShapeDtypeStruct((blocks, row_count, HEADS // blocks, HD), jnp.bfloat16),
            pltpu.VMEM((LEAD, weight.shape[0], TILE), jnp.bfloat16),
        ),
        in_specs=[pl.BlockSpec(memory_space=pltpu.SMEM)] + [vmem] * 3 + [hbm] * 3,
        out_specs=(vmem, vmem),
        scratch_shapes=[pltpu.VMEM((slots, width), jnp.bfloat16)] * (2 * row_count)
        + [pltpu.SemaphoreType.DMA((2 * row_count + LEAD,))],
        compiler_params=pltpu.CompilerParams(vmem_limit_bytes=32 * 2**20),
        cost_estimate=pl.CostEstimate(
            flops=4 * row_count * HEADS * slots * HD,
            bytes_accessed=4 * row_count * slots * width,
            transcendentals=row_count * HEADS * slots,
        ),
        name="attend",
    )(lengths, query, keyval, turn, key_cache, value_cache, weight)


def arrange(core_ref, mine_ref, other_ref, out_ref, wide_ref):
    sources, row_count, heads, _ = mine_ref.shape
    core = core_ref[0]
    shape = (sources, row_count * heads, HD)
    wide_ref[:, core] = mine_ref[...].astype(jnp.float32).reshape(shape)
    wide_ref[:, 1 - core] = other_ref[...].astype(jnp.float32).reshape(shape)
    flat = wide_ref.reshape(sources * 2 * row_count * heads, HD)
    for g in range(heads):
        rows = flat[pl.ds(g, sources * 2 * row_count, stride=heads), :]
        out_ref[:, g * HD:(g + 1) * HD] = rows.astype(jnp.bfloat16)


def arrangement(core, mine, other):
    sources, row_count, heads, width = mine.shape
    if heads % 16:
        both = jnp.stack(
            [jnp.where(core[0] == 0, mine, other), jnp.where(core[0] == 0, other, mine)], axis=1
        )
        return both.reshape(sources * 2 * row_count, heads * width)
    vmem = pl.BlockSpec(memory_space=pltpu.VMEM)
    return pl.pallas_call(
        arrange,
        out_shape=jax.ShapeDtypeStruct((sources * 2 * row_count, heads * width), jnp.bfloat16),
        in_specs=[pl.BlockSpec(memory_space=pltpu.SMEM), vmem, vmem],
        out_specs=vmem,
        scratch_shapes=[pltpu.VMEM((sources, 2, row_count * heads, width), jnp.float32)],
        compiler_params=pltpu.CompilerParams(vmem_limit_bytes=8 * 2**20),
        name="arrange",
    )(core, mine, other)


def project(first, lead, place_ref, rows_ref, weight_hbm, *rest):
    product_ref, weight_buf, weight_sem = rest[-3:]
    own_ref, *send_refs = rest[-3 - NEAR:-3]
    blocks = product_ref.shape[0]
    tiles = lead + weight_buf.shape[0]
    weights = [rest[0].at[j] for j in range(lead)] + [weight_buf.at[j] for j in range(tiles - lead)]
    copies = [None] * lead
    for j in range(lead, tiles):
        columns = pl.ds((first + j) * TILE, TILE)
        copies.append(pltpu.make_async_copy(weight_hbm.at[:, columns], weights[j], weight_sem.at[j - lead]))
        copies[-1].start()
    place = place_ref[0]
    for j in range(tiles):
        columns = slice(j * TILE, (j + 1) * TILE)
        if copies[j] is not None:
            copies[j].wait()
        product = jnp.dot(rows_ref[...], weights[j][...], preferred_element_type=jnp.float32)
        product_ref[:, :, columns] = product.reshape(blocks, -1, TILE)
        for step in range(NEAR):
            taken = jnp.concatenate(
                [product_ref[NEAR * far + (place ^ step), :, columns] for far in range(blocks // NEAR)], axis=0
            )
            if step:
                send_refs[step - 1][:, columns] = taken.astype(jnp.bfloat16)
            else:
                own_ref[:, columns] = taken


def projection(place, rows, weight, lead, first, count, blocks):
    row_count, depth = rows.shape
    out_rows = row_count // NEAR
    leads = len(lead) and lead[0].shape[0]
    vmem = pl.BlockSpec(memory_space=pltpu.VMEM)
    shapes = [jax.ShapeDtypeStruct((out_rows, count * TILE), jnp.float32)]
    shapes += [jax.ShapeDtypeStruct((out_rows, count * TILE), jnp.bfloat16)] * (NEAR - 1)
    return pl.pallas_call(
        functools.partial(project, first, leads),
        out_shape=shapes,
        in_specs=[pl.BlockSpec(memory_space=pltpu.SMEM), vmem, pl.BlockSpec(memory_space=pltpu.HBM)] + [vmem] * len(lead),
        out_specs=[vmem] * NEAR,
        scratch_shapes=[
            pltpu.VMEM((blocks, row_count // blocks, count * TILE), jnp.float32),
            pltpu.VMEM((count - leads, depth, TILE), jnp.bfloat16),
            pltpu.SemaphoreType.DMA((count - leads,)),
        ],
        compiler_params=pltpu.CompilerParams(vmem_limit_bytes=40 * 2**20),
        cost_estimate=pl.CostEstimate(
            flops=2 * row_count * depth * count * TILE,
            bytes_accessed=2 * depth * count * TILE,
            transcendentals=0,
        ),
        name="project",
    )(place, rows, pltpu.with_memory_space_constraint(weight, pltpu.HBM), *(pltpu.with_memory_space_constraint(w, pltpu.VMEM) for w in lead))


def shards(residual, query, new_keyval, key_cache, value_cache, lengths, out_weight):
    gx_count = lax.axis_size("gx")
    gx_index = lax.axis_index("gx")
    row_count = lengths.shape[0]
    query_width = query.shape[1]

    both = jnp.concatenate([query, new_keyval], axis=1).reshape(-1, row_count, query_width + new_keyval.shape[1])
    both = lax.all_to_all(both, ("gx", "gy"), split_axis=0, concat_axis=0, tiled=True)
    both = both.transpose(1, 0, 2)
    query_rows = both[:, :, :query_width].reshape(row_count, HEADS, HD)
    keyval_rows = both[:, :, query_width:].reshape(row_count, 2 * KV_HEADS, HD)

    frequency = ROPE_BASE ** (-2.0 * np.arange(HD // 2) / HD)
    frequency = np.concatenate([frequency, frequency]).astype(np.float32)
    side = np.where(np.arange(HD) < HD // 2, -1.0, 1.0).astype(np.float32)
    angles = lengths.astype(jnp.float32)[:, None] * frequency[None, :]
    turn = jnp.stack([jnp.cos(angles), jnp.sin(angles) * side], axis=1)

    bounded = jnp.minimum(lengths, key_cache.shape[1] - 1)
    near_place = jnp.reshape(gx_index % NEAR, (1,)).astype(jnp.int32)
    far_place = gx_index // NEAR
    far_count = gx_count // NEAR
    core = jnp.reshape(lax.axis_index("gy"), (1,)).astype(jnp.int32)
    bounded, near_place, far_place, core = lax.optimization_barrier((bounded, near_place, far_place, core))
    tiles = out_weight.shape[1] // TILE
    counts = [int(round(tiles * share)) for share in CHUNKS]
    mixed, lead = attention(
        bounded, query_rows, keyval_rows, turn, key_cache, value_cache, out_weight, tiles - counts[-1], gx_count
    )
    mixed, near_place, far_place, core = lax.optimization_barrier((mixed, near_place, far_place, core))
    mixed = lax.all_to_all(mixed, "gx", split_axis=0, concat_axis=0, tiled=True)
    other = lax.ppermute(mixed, "gy", [(0, 1), (1, 0)])
    feature_rows = arrangement(core, mixed, other)
    block_rows = feature_rows.shape[0] // gx_count
    starts = [sum(counts[:i]) for i in range(len(counts))]
    outs = []
    earlier = None
    leads = [lead]
    for first, count in reversed(list(zip(starts, counts))):
        columns = slice(first * TILE, (first + count) * TILE)
        own, *sends = projection(near_place, feature_rows, out_weight, leads, first, count, gx_count)
        leads = []
        if earlier is not None:
            own, earlier = lax.optimization_barrier((own, earlier))
        total = own
        for step, send in enumerate(sends, 1):
            got = lax.ppermute(send, "gx", [(i, i ^ step) for i in range(gx_count)])
            total = total + got.astype(jnp.float32)
        total = total.reshape(far_count, block_rows, count * TILE)
        if far_count == 2:
            low, high = total[0], total[1]
            mine = jnp.where(far_place == 0, low, high)
            send = jnp.where(far_place == 0, high, low).astype(jnp.bfloat16)
            got = lax.ppermute(send, "gx", [(i, i ^ NEAR) for i in range(gx_count)])
            earlier = got
            summed = mine + got.astype(jnp.float32)
        elif far_count > 1:
            parts = [[near + NEAR * far for far in range(far_count)] for near in range(NEAR)]
            got = lax.all_to_all(
                total.astype(jnp.bfloat16), "gx", split_axis=0, concat_axis=0,
                axis_index_groups=parts, tiled=True,
            )
            summed = jnp.sum(got.astype(jnp.float32), axis=0)
        else:
            summed = total[0]
        outs.append((residual[:, columns].astype(jnp.float32) + summed).astype(jnp.bfloat16))
    return jnp.concatenate(outs[::-1], axis=1)


def solution(mesh):
    in_specs = (
        P(("groups", "gx"), "gy"),
        P("groups", ("gx", "gy")),
        P("groups", ("gx", "gy")),
        P(("groups", "gx", "gy"), None, None),
        P(("groups", "gx", "gy"), None, None),
        P(("groups", "gx", "gy")),
        P("gx", "gy"),
    )
    out_specs = P(("groups", "gx"), "gy")
    return jax.shard_map(shards, mesh=mesh, in_specs=in_specs, out_specs=out_specs, check_vma=False)
```

```python
import functools
import math

import jax
import jax.numpy as jnp
import numpy as np
from jax import lax
from jax.experimental import pallas as pl
from jax.experimental.pallas import tpu as pltpu
from jax.sharding import PartitionSpec as P

HEADS = 128
KV_HEADS = 8
HD = 128
GROUP = HEADS // KV_HEADS
ROPE_BASE = 500000.0
NORM = 1.0 / math.sqrt(HD)
MIX_NORM = 1.0 / math.sqrt(HEADS)
CHUNKS = (0.375, 0.625)
NEAR = 4
TILE = 512
LEAD = 4


def sign_table(order):
    bits = lax.broadcasted_iota(jnp.int32, (order, order), 0) & lax.broadcasted_iota(jnp.int32, (order, order), 1)
    step = 1
    while step < order.bit_length():
        step *= 2
    while step > 1:
        step //= 2
        bits = bits ^ (bits >> step)
    return (1 - 2 * (bits & 1)).astype(jnp.float32).astype(jnp.bfloat16)


def hadamard(rows, table):
    high = rows.astype(jnp.bfloat16)
    rest = rows - high.astype(jnp.float32)
    middle = rest.astype(jnp.bfloat16)
    low = (rest - middle.astype(jnp.float32)).astype(jnp.bfloat16)
    dot = functools.partial(jnp.dot, preferred_element_type=jnp.float32)
    return (dot(high, table) + (dot(middle, table) + dot(low, table))) * NORM


def put_row(buf, length, rows):
    base = pl.multiple_of((length >> 4) << 4, 16)
    here = lax.broadcasted_iota(jnp.int32, (16, HD), 0) == length - base
    for k in range(KV_HEADS):
        lanes = slice(k * HD, (k + 1) * HD)
        old = buf[pl.ds(base, 16), lanes].astype(jnp.float32)
        buf[pl.ds(base, 16), lanes] = jnp.where(here, rows[k:k + 1], old).astype(jnp.bfloat16)


def attend(
    first, lengths_ref, query_ref, keyval_ref, turn_ref, key_hbm, value_hbm, weight_hbm,
    out_ref, lead_ref, *scratch,
):
    row_count = lengths_ref.shape[0]
    key_bufs, value_bufs = scratch[:row_count], scratch[row_count:2 * row_count]
    sem = scratch[-1]
    slots = key_bufs[0].shape[0]
    requests = range(row_count)
    key_copies = [pltpu.make_async_copy(key_hbm.at[r], key_bufs[r], sem.at[r]) for r in requests]
    value_copies = [pltpu.make_async_copy(value_hbm.at[r], value_bufs[r], sem.at[row_count + r]) for r in requests]
    lead_copies = [
        pltpu.make_async_copy(
            weight_hbm.at[:, pl.ds((first + j) * TILE, TILE)], lead_ref.at[j], sem.at[2 * row_count + j]
        )
        for j in range(lead_ref.shape[0])
    ]
    for copy in key_copies + value_copies + lead_copies:
        copy.start()
    table = sign_table(HD)
    turned = []
    for r in requests:
        cos, sin = turn_ref[r, 0:1, :], turn_ref[r, 1:2, :]
        for vector in (query_ref[r].astype(jnp.float32), keyval_ref[r].astype(jnp.float32)):
            turned.append(vector * cos + pltpu.roll(vector, HD // 2, axis=1) * sin)
    turned = hadamard(jnp.concatenate(turned, axis=0), table)
    stride = HEADS + 2 * KV_HEADS
    head_of = lax.broadcasted_iota(jnp.int32, (HD, HEADS), 1) // GROUP
    spread = []
    for r in requests:
        across = jnp.transpose(turned[r * stride:r * stride + HEADS])
        spread.append(jnp.concatenate(
            [jnp.where(head_of == k, across, 0.0).astype(jnp.bfloat16) for k in range(KV_HEADS)], axis=0
        ))
    for r in requests:
        key_copies[r].wait()
        put_row(key_bufs[r], lengths_ref[r], turned[r * stride + HEADS:r * stride + HEADS + KV_HEADS])
    slot = lax.broadcasted_iota(jnp.int32, (slots, HEADS), 0)
    weights = []
    for r in requests:
        scores = jnp.dot(key_bufs[r][...], spread[r], preferred_element_type=jnp.float32) * NORM
        scores = jnp.where(slot <= lengths_ref[r], scores, -jnp.inf)
        lifted = jnp.exp(scores - jnp.max(scores, axis=0, keepdims=True))
        lifted = lifted * (1.0 / jnp.sum(lifted, axis=0, keepdims=True))
        weights.append(jnp.transpose(lifted.astype(jnp.bfloat16)))
    for r in requests:
        value_copies[r].wait()
        put_row(value_bufs[r], lengths_ref[r], keyval_ref[r, KV_HEADS:].astype(jnp.float32))
    for r in requests:
        attended = []
        for k in range(0, KV_HEADS, 2):
            two = jnp.dot(
                weights[r][k * GROUP:(k + 2) * GROUP], value_bufs[r][:, k * HD:(k + 2) * HD],
                preferred_element_type=jnp.float32,
            )
            attended += [two[:GROUP, :HD], two[GROUP:, HD:]]
        attended = jnp.concatenate(attended, axis=0).astype(jnp.bfloat16)
        mixed = jnp.dot(table, attended, preferred_element_type=jnp.float32) * MIX_NORM
        out_ref[:, r] = mixed.reshape(out_ref.shape[0], *out_ref.shape[2:]).astype(jnp.bfloat16)
    for copy in lead_copies:
        copy.wait()


def attention(lengths, query, keyval, turn, key_cache, value_cache, weight, first, blocks):
    row_count, slots, width = key_cache.shape
    vmem, hbm = pl.BlockSpec(memory_space=pltpu.VMEM), pl.BlockSpec(memory_space=pltpu.HBM)
    key_cache = pltpu.with_memory_space_constraint(key_cache, pltpu.HBM)
    value_cache = pltpu.with_memory_space_constraint(value_cache, pltpu.HBM)
    weight = pltpu.with_memory_space_constraint(weight, pltpu.HBM)
    return pl.pallas_call(
        functools.partial(attend, first),
        out_shape=(
            jax.ShapeDtypeStruct((blocks, row_count, HEADS // blocks, HD), jnp.bfloat16),
            pltpu.VMEM((LEAD, weight.shape[0], TILE), jnp.bfloat16),
        ),
        in_specs=[pl.BlockSpec(memory_space=pltpu.SMEM)] + [vmem] * 3 + [hbm] * 3,
        out_specs=(vmem, vmem),
        scratch_shapes=[pltpu.VMEM((slots, width), jnp.bfloat16)] * (2 * row_count)
        + [pltpu.SemaphoreType.DMA((2 * row_count + LEAD,))],
        compiler_params=pltpu.CompilerParams(vmem_limit_bytes=32 * 2**20),
        cost_estimate=pl.CostEstimate(
            flops=4 * row_count * HEADS * slots * HD,
            bytes_accessed=4 * row_count * slots * width,
            transcendentals=row_count * HEADS * slots,
        ),
        name="attend",
    )(lengths, query, keyval, turn, key_cache, value_cache, weight)


def arrange(core_ref, mine_ref, other_ref, out_ref, wide_ref):
    sources, row_count, heads, _ = mine_ref.shape
    core = core_ref[0]
    shape = (sources, row_count * heads, HD)
    wide_ref[:, core] = mine_ref[...].astype(jnp.float32).reshape(shape)
    wide_ref[:, 1 - core] = other_ref[...].astype(jnp.float32).reshape(shape)
    flat = wide_ref.reshape(sources * 2 * row_count * heads, HD)
    for g in range(heads):
        rows = flat[pl.ds(g, sources * 2 * row_count, stride=heads), :]
        out_ref[:, g * HD:(g + 1) * HD] = rows.astype(jnp.bfloat16)


def arrangement(core, mine, other):
    sources, row_count, heads, width = mine.shape
    if heads % 16:
        both = jnp.stack(
            [jnp.where(core[0] == 0, mine, other), jnp.where(core[0] == 0, other, mine)], axis=1
        )
        return both.reshape(sources * 2 * row_count, heads * width)
    vmem = pl.BlockSpec(memory_space=pltpu.VMEM)
    return pl.pallas_call(
        arrange,
        out_shape=jax.ShapeDtypeStruct((sources * 2 * row_count, heads * width), jnp.bfloat16),
        in_specs=[pl.BlockSpec(memory_space=pltpu.SMEM), vmem, vmem],
        out_specs=vmem,
        scratch_shapes=[pltpu.VMEM((sources, 2, row_count * heads, width), jnp.float32)],
        compiler_params=pltpu.CompilerParams(vmem_limit_bytes=8 * 2**20),
        name="arrange",
    )(core, mine, other)


def project(first, lead, place_ref, rows_ref, weight_hbm, *rest):
    product_ref, weight_buf, weight_sem = rest[-3:]
    own_ref, *send_refs = rest[-3 - NEAR:-3]
    blocks = product_ref.shape[0]
    tiles = lead + weight_buf.shape[0]
    weights = [rest[0].at[j] for j in range(lead)] + [weight_buf.at[j] for j in range(tiles - lead)]
    copies = [None] * lead
    for j in range(lead, tiles):
        columns = pl.ds((first + j) * TILE, TILE)
        copies.append(pltpu.make_async_copy(weight_hbm.at[:, columns], weights[j], weight_sem.at[j - lead]))
        copies[-1].start()
    place = place_ref[0]
    for j in range(tiles):
        columns = slice(j * TILE, (j + 1) * TILE)
        if copies[j] is not None:
            copies[j].wait()
        product = jnp.dot(rows_ref[...], weights[j][...], preferred_element_type=jnp.float32)
        product_ref[:, :, columns] = product.reshape(blocks, -1, TILE)
        for step in range(NEAR):
            taken = jnp.concatenate(
                [product_ref[NEAR * far + (place ^ step), :, columns] for far in range(blocks // NEAR)], axis=0
            )
            if step:
                send_refs[step - 1][:, columns] = taken.astype(jnp.bfloat16)
            else:
                own_ref[:, columns] = taken


def projection(place, rows, weight, lead, first, count, blocks):
    row_count, depth = rows.shape
    out_rows = row_count // NEAR
    leads = len(lead) and lead[0].shape[0]
    vmem = pl.BlockSpec(memory_space=pltpu.VMEM)
    shapes = [jax.ShapeDtypeStruct((out_rows, count * TILE), jnp.float32)]
    shapes += [jax.ShapeDtypeStruct((out_rows, count * TILE), jnp.bfloat16)] * (NEAR - 1)
    return pl.pallas_call(
        functools.partial(project, first, leads),
        out_shape=shapes,
        in_specs=[pl.BlockSpec(memory_space=pltpu.SMEM), vmem, pl.BlockSpec(memory_space=pltpu.HBM)] + [vmem] * len(lead),
        out_specs=[vmem] * NEAR,
        scratch_shapes=[
            pltpu.VMEM((blocks, row_count // blocks, count * TILE), jnp.float32),
            pltpu.VMEM((count - leads, depth, TILE), jnp.bfloat16),
            pltpu.SemaphoreType.DMA((count - leads,)),
        ],
        compiler_params=pltpu.CompilerParams(vmem_limit_bytes=40 * 2**20),
        cost_estimate=pl.CostEstimate(
            flops=2 * row_count * depth * count * TILE,
            bytes_accessed=2 * depth * count * TILE,
            transcendentals=0,
        ),
        name="project",
    )(place, rows, pltpu.with_memory_space_constraint(weight, pltpu.HBM), *(pltpu.with_memory_space_constraint(w, pltpu.VMEM) for w in lead))


def shards(residual, query, new_keyval, key_cache, value_cache, lengths, out_weight):
    gx_count = lax.axis_size("gx")
    gx_index = lax.axis_index("gx")
    row_count = lengths.shape[0]
    query_width = query.shape[1]

    both = jnp.concatenate([query, new_keyval], axis=1).reshape(-1, row_count, query_width + new_keyval.shape[1])
    both = lax.all_to_all(both, ("gx", "gy"), split_axis=0, concat_axis=0, tiled=True)
    both = both.transpose(1, 0, 2)
    query_rows = both[:, :, :query_width].reshape(row_count, HEADS, HD)
    keyval_rows = both[:, :, query_width:].reshape(row_count, 2 * KV_HEADS, HD)

    frequency = ROPE_BASE ** (-2.0 * np.arange(HD // 2) / HD)
    frequency = np.concatenate([frequency, frequency]).astype(np.float32)
    side = np.where(np.arange(HD) < HD // 2, -1.0, 1.0).astype(np.float32)
    angles = lengths.astype(jnp.float32)[:, None] * frequency[None, :]
    turn = jnp.stack([jnp.cos(angles), jnp.sin(angles) * side], axis=1)

    bounded = jnp.minimum(lengths, key_cache.shape[1] - 1)
    near_place = jnp.reshape(gx_index % NEAR, (1,)).astype(jnp.int32)
    far_place = gx_index // NEAR
    far_count = gx_count // NEAR
    core = jnp.reshape(lax.axis_index("gy"), (1,)).astype(jnp.int32)
    bounded, near_place, far_place, core = lax.optimization_barrier((bounded, near_place, far_place, core))
    tiles = out_weight.shape[1] // TILE
    counts = [int(round(tiles * share)) for share in CHUNKS]
    mixed, lead = attention(
        bounded, query_rows, keyval_rows, turn, key_cache, value_cache, out_weight, tiles - counts[-1], gx_count
    )
    mixed, near_place, far_place, core = lax.optimization_barrier((mixed, near_place, far_place, core))
    mixed = lax.all_to_all(mixed, "gx", split_axis=0, concat_axis=0, tiled=True)
    other = lax.ppermute(mixed, "gy", [(0, 1), (1, 0)])
    feature_rows = arrangement(core, mixed, other)
    block_rows = feature_rows.shape[0] // gx_count
    starts = [sum(counts[:i]) for i in range(len(counts))]
    outs = []
    earlier = None
    leads = [lead]
    for first, count in reversed(list(zip(starts, counts))):
        columns = slice(first * TILE, (first + count) * TILE)
        own, *sends = projection(near_place, feature_rows, out_weight, leads, first, count, gx_count)
        leads = []
        if earlier is not None:
            own, earlier = lax.optimization_barrier((own, earlier))
        total = own
        for step in (3, 1, 2):
            send = sends[step - 1]
            got = lax.ppermute(send, "gx", [(i, i ^ step) for i in range(gx_count)])
            total = total + got.astype(jnp.float32)
        total = total.reshape(far_count, block_rows, count * TILE)
        if far_count == 2:
            low, high = total[0], total[1]
            mine = jnp.where(far_place == 0, low, high)
            send = jnp.where(far_place == 0, high, low).astype(jnp.bfloat16)
            got = lax.ppermute(send, "gx", [(i, i ^ NEAR) for i in range(gx_count)])
            earlier = got
            summed = mine + got.astype(jnp.float32)
        elif far_count > 1:
            parts = [[near + NEAR * far for far in range(far_count)] for near in range(NEAR)]
            got = lax.all_to_all(
                total.astype(jnp.bfloat16), "gx", split_axis=0, concat_axis=0,
                axis_index_groups=parts, tiled=True,
            )
            summed = jnp.sum(got.astype(jnp.float32), axis=0)
        else:
            summed = total[0]
        outs.append((residual[:, columns].astype(jnp.float32) + summed).astype(jnp.bfloat16))
    return jnp.concatenate(outs[::-1], axis=1)


def solution(mesh):
    in_specs = (
        P(("groups", "gx"), "gy"),
        P("groups", ("gx", "gy")),
        P("groups", ("gx", "gy")),
        P(("groups", "gx", "gy"), None, None),
        P(("groups", "gx", "gy"), None, None),
        P(("groups", "gx", "gy")),
        P("gx", "gy"),
    )
    out_specs = P(("groups", "gx"), "gy")
    return jax.shard_map(shards, mesh=mesh, in_specs=in_specs, out_specs=out_specs, check_vma=False)
```
